32 devices in a mesh: seq: 8 (over y, x, core), vis: 4 (over z).
Axes of the slice: x: 2, y: 2, z: 4, core: 2. Of those that a mesh axis runs over, the one named last changes fastest.
Arguments:
- text: bfloat16 [2048, 8192], P('seq'), may hold values from -6 to 6
- frames: bfloat16 [2048, 8192], P(('seq', 'vis')), may hold values from -60 to 60
- tile_pos: int32 [2048], P(('seq', 'vis')), may hold values from 0 to 2047, as said below
- frame_count: int32 [32], P(('seq', 'vis')), may hold values from 8 to 64
- doc_ids: int32 [2048], replicated, may hold values from 0 to 3, never falling along the last dimension, each value on 1 to 1024 neighbouring positions
- norm_gain: float32 [8192], replicated, may hold values from 0.1 to 1.9
- w_query: bfloat16 [8192, 8192], P(None, 'vis'), may hold values from -4 to 4
- q_bias: float32 [8192], P('vis'), may hold values from -3 to 3
- w_key: bfloat16 [8192, 1024], P(None, 'vis'), may hold values from -4 to 4
- w_value: bfloat16 [8192, 1024], P(None, 'vis'), may hold values from -0.0625 to 0.0625
- v_bias: float32 [1024], P('vis'), may hold values from -3 to 3
Outputs:
- attended: bfloat16 [2048, 8192], P('seq', 'vis')
The draws below stay inside these ranges and needn't reach their ends.
Inputs may be any that keep to these rules, and one draw needn't show every extreme that they name: `tile_pos`: all entries together name every position of the window once. Of one device's 64 rows, at most 8 of those below its frame_count fall into one shard of 256 positions, and in every draw one shard receives exactly 8 usable rows from every device. Rows at or beyond the count are unused. `doc_ids`: never falling along the window.
All inputs are finite; a program needn't handle non-finite values.
Results may differ from the reference program's by a relative error of at most 0.0069.
Values may be sent and summed in bfloat16 or wider, within the bound.
No kernel may reach another device: no remote copies, remote signals or barrier semaphores. Data moves between devices by JAX's collectives and lax.ppermute only.
A program may use at most 128 MiB of HBM per device.

```python
import math
import jax
import jax.numpy as jnp
import numpy as np
from jax import lax

D = 8192
HEADS = 64
KV_HEADS = 8
HEAD_DIM = 128
DOCS = 4
TOK_DEV = 256
QPG = 8
TOKENS = 2048
CAP = 8
F_DEV = 64
N_SEQ = 8
N_VIS = 4


def permute_rows(seeds, length):

    def permute_one(seed_key):
        return jax.random.permutation(seed_key, length)
    return jax.vmap(permute_one)(seeds)


def tile_layout(key):
    devices = N_SEQ * N_VIS
    slots = N_SEQ * CAP
    folded = jax.random.fold_in(key, 71)
    key_counts, key_owner, key_busy, key_quiet, key_windows, key_order = jax.random.split(folded, 6)
    counts = jax.random.randint(key_counts, (devices, N_SEQ), 0, CAP + 1)
    full_owner = jax.random.randint(key_owner, (), 0, N_SEQ)
    owner_ids = jnp.arange(N_SEQ)[None, :]
    device_ids = jnp.arange(devices)[:, None]
    busiest = jax.random.randint(key_busy, (), 0, devices)
    quietest = (busiest + 1 + jax.random.randint(key_quiet, (), 0, devices - 1)) % devices
    counts = jnp.where(owner_ids == full_owner, CAP, counts)
    counts = jnp.where(device_ids == busiest, CAP, counts)
    counts = jnp.where((device_ids == quietest) & (owner_ids != full_owner), 0, counts)
    windows = permute_rows(jax.random.split(key_windows, N_SEQ), devices)
    offsets = jnp.arange(CAP)[None, None, :]
    places = jnp.arange(N_SEQ)[None, :, None] * TOK_DEV + windows.T[:, :, None] * CAP + offsets
    usable = (offsets < counts[:, :, None]).reshape(devices, slots)
    shuffle = permute_rows(jax.random.split(key_order, devices), slots)
    sort_keys = jnp.where(usable, 0, slots) + shuffle
    order = jnp.argsort(sort_keys, axis=1)
    placed = jnp.take_along_axis(places.reshape(devices, slots), order, axis=1)
    return (placed.reshape(devices * slots).astype(jnp.int32), jnp.sum(counts, axis=1).astype(jnp.int32))


def draw_tile_pos(key, part):
    return tile_layout(key)[0]


def draw_frame_count(key, part):
    return tile_layout(key)[1]


def draw_frames(key, part):
    base = jax.random.normal(jax.random.fold_in(key, 5), (TOKENS, D), jnp.float32)
    return jnp.clip(base, -60.0, 60.0).astype(jnp.bfloat16)


def draw_w_key(key, part):
    matrix = jax.random.normal(jax.random.fold_in(key, 31), (D, KV_HEADS * HEAD_DIM), jnp.float32) / math.sqrt(D)
    return jnp.clip(matrix, -4.0, 4.0).astype(jnp.bfloat16)


def draw_w_query(key, part):
    matrix = jax.random.normal(jax.random.fold_in(key, 37), (D, HEADS * HEAD_DIM), jnp.float32) * (2.0 / math.sqrt(D))
    return jnp.clip(matrix, -4.0, 4.0).astype(jnp.bfloat16)


def steps_of(stream_key, shape, cuts, least, top_value):
    factor_of = 1.0
    for dim, parts in cuts:
        heights = jax.random.uniform(jax.random.fold_in(jax.random.fold_in(stream_key, 6), dim), (parts,), jnp.float32, least / len(cuts), top_value / len(cuts))
        factor_of = factor_of * jnp.repeat(jnp.exp(heights), shape[dim] // parts).reshape((-1,) + (1,) * (len(shape) - 1 - dim))
    return factor_of


def split_up(count, total, limit, slope):
    loads = [(1 << 20) // math.isqrt(rank ** slope) + 1 for rank in range(2, count + 1)]
    surplus, holding = total - limit - (count - 1), [1] * (count - 1)
    while surplus > 0:
        movable = [i for i in range(count - 1) if holding[i] < limit]
        mass, budget = sum([loads[i] for i in movable]), surplus
        for i in movable:
            addition = min(limit - holding[i], max(1, budget * loads[i] // mass), surplus)
            holding[i] = holding[i] + addition
            surplus = surplus - addition
    return np.array([limit] + holding)


def uneven(rng, count, total, limit, slope):
    if count == 2:
        one = jax.random.randint(rng, (), max(1, total - limit), min(limit, total - 1) + 1)
        return jnp.stack([one, total - one])
    tallies = jnp.asarray(split_up(count, total, limit, slope), jnp.int32)
    couples = (count - 1) // 2
    giver, sink = tallies[1:1 + 2 * couples:2], tallies[2:2 + 2 * couples:2]
    slack = jnp.minimum(giver - 1, limit - sink)
    moved = jax.random.randint(jax.random.fold_in(rng, 1), (couples,), 0, 1 << 20) % (slack + 1)
    tallies = tallies.at[1:1 + 2 * couples:2].set(giver - moved).at[2:2 + 2 * couples:2].set(sink + moved)
    return tallies[jax.random.permutation(jax.random.fold_in(rng, 2), count)]


def bell_draw(own_key, shape, deviation, reach, cuts=(), held_as=jnp.bfloat16):
    loudness = steps_of(own_key, shape, cuts, -0.22, 0.18) if cuts else 1.0
    values = jax.random.normal(own_key, shape, jnp.float32) * deviation * loudness
    return jnp.minimum(jnp.maximum(values, -reach), reach).astype(held_as)


def setup_inputs(seed: int = 0) -> dict:
    key_of = jax.random.split(jax.random.key(seed), 12)
    text = bell_draw(key_of[0], (TOKENS, D), 1.0, 6.0, ((0, 8),))
    frames = draw_frames(jax.random.fold_in(key_of[11], 71), 0)
    tile_pos = draw_tile_pos(jax.random.fold_in(key_of[11], 71), 0)
    frame_count = draw_frame_count(jax.random.fold_in(key_of[11], 71), 0)
    doc_ids = jnp.searchsorted(jnp.cumsum(uneven(key_of[4], DOCS, TOKENS, TOKENS // 2, 2)), jnp.arange(TOKENS), side="right").astype(jnp.int32)
    norm_gain = jnp.clip(1.0 + 0.18 * jax.random.normal(key_of[5], (D,), jnp.float32), 0.1, 1.9)
    w_query = draw_w_query(jax.random.fold_in(key_of[11], 71), 0)
    q_bias = bell_draw(key_of[7], (HEADS * HEAD_DIM,), 0.5, 3.0, ((0, 4),), jnp.float32)
    w_key = draw_w_key(jax.random.fold_in(key_of[11], 71), 0)
    w_value = bell_draw(key_of[9], (D, KV_HEADS * HEAD_DIM), D ** -0.5, 0.0625, ((1, 4),))
    v_bias = bell_draw(key_of[10], (KV_HEADS * HEAD_DIM,), 0.5, 3.0, ((0, 4),), jnp.float32)
    return {"text": text, "frames": frames, "tile_pos": tile_pos, "frame_count": frame_count, "doc_ids": doc_ids, "norm_gain": norm_gain, "w_query": w_query, "q_bias": q_bias, "w_key": w_key, "w_value": w_value, "v_bias": v_bias}


epsilon = 1e-06

def reference(text, frames, tile_pos, frame_count, doc_ids, norm_gain, w_query, q_bias, w_key, w_value, v_bias):
    usable = (jnp.arange(F_DEV, dtype=jnp.int32)[None, :] < frame_count[:, None]).reshape(TOKENS)
    target = jnp.where(usable, tile_pos, TOKENS).astype(jnp.int32)
    merged = text.at[target].set(frames, mode='drop')
    widened = merged.astype(jnp.float32)
    mean_square = lax.optimization_barrier(jnp.mean(widened * widened, axis=1, keepdims=True))
    normed = (widened * lax.rsqrt(mean_square + epsilon) * norm_gain).astype(jnp.bfloat16)
    queries = (jnp.dot(normed, w_query, preferred_element_type=jnp.float32) + q_bias).astype(jnp.bfloat16)
    key_rows = jnp.dot(normed, w_key, preferred_element_type=jnp.float32).astype(jnp.bfloat16)
    values = (jnp.dot(normed, w_value, preferred_element_type=jnp.float32) + v_bias).astype(jnp.bfloat16)
    query_groups = queries.reshape(TOKENS, KV_HEADS, QPG, HEAD_DIM).transpose(1, 0, 2, 3)
    key_groups = key_rows.reshape(TOKENS, KV_HEADS, HEAD_DIM).transpose(1, 0, 2)
    value_groups = values.reshape(TOKENS, KV_HEADS, HEAD_DIM).transpose(1, 0, 2)
    block_rows = min(512, TOKENS)
    positions = jnp.arange(TOKENS, dtype=jnp.int32)
    score_scale = HEAD_DIM ** (-0.5)

    def one_group(operands):
        query_group, key_group, value_group = operands
        key_wide = key_group.astype(jnp.float32)
        value_wide = value_group.astype(jnp.float32)

        def one_block(block_index):
            row_start = (block_index * block_rows).astype(jnp.int32)
            query_block = lax.dynamic_slice_in_dim(query_group, row_start, block_rows, 0).astype(jnp.float32)
            query_place = row_start + jnp.arange(block_rows, dtype=jnp.int32)
            query_docs = lax.dynamic_slice_in_dim(doc_ids, row_start, block_rows, 0)
            scores = jnp.einsum('qjd,kd->qjk', query_block, key_wide) * score_scale
            allowed = (positions[None, :] <= query_place[:, None]) & (doc_ids[None, :] == query_docs[:, None])
            allowed = allowed[:, None, :]
            row_peak = lax.optimization_barrier(jnp.max(jnp.where(allowed, scores, -jnp.inf), axis=2, keepdims=True))
            raised = jnp.where(allowed, jnp.exp(scores - row_peak), 0.0)
            row_total = lax.optimization_barrier(jnp.sum(raised, axis=2))
            weights = raised.astype(jnp.bfloat16)
            summed = jnp.einsum('qjk,kd->qjd', weights.astype(jnp.float32), value_wide)
            return (summed / row_total[:, :, None]).astype(jnp.bfloat16)
        outputs = lax.map(one_block, jnp.arange(TOKENS // block_rows, dtype=jnp.int32))
        return outputs.reshape(TOKENS, QPG, HEAD_DIM)
    result = lax.map(one_group, (query_groups, key_groups, value_groups))
    return result.transpose(1, 0, 2, 3).reshape(TOKENS, HEADS * HEAD_DIM)
```

```python
import functools

import jax
import jax.numpy as jnp
from jax import lax
from jax.experimental import pallas as pl
from jax.experimental.pallas import tpu as pltpu
from jax.sharding import PartitionSpec as P

HEAD_DIM = 128
META = 128
CHUNKS = 4
EPSILON = 1e-06
NEGATIVE = -1e30
VMEM_LIMIT = 48 * 1024 * 1024
F32 = jnp.float32
BF16 = jnp.bfloat16


def params(limit=VMEM_LIMIT):
    return pltpu.CompilerParams(vmem_limit_bytes=limit)


def cost(flops, moved):
    return pl.CostEstimate(flops=int(flops), bytes_accessed=int(moved), transcendentals=0)


def normed_rows(rows, gain):
    widened = rows.astype(F32)
    mean_square = jnp.mean(widened * widened, axis=1, keepdims=True)
    return (widened * lax.rsqrt(mean_square + EPSILON) * gain).astype(BF16)


def slots_kernel(scalars, frames, gain, place_row, first, rest, *, shard_rows, capacity):
    count, shard = scalars[0], scalars[1]
    rows, width = frames.shape
    across = lax.broadcasted_iota(jnp.int32, (rows, rows), 1)
    down = lax.broadcasted_iota(jnp.int32, (rows, rows), 0)
    places = jnp.broadcast_to(place_row[...], (rows, rows))
    place_column = jnp.sum(jnp.where(down == across, places, 0), axis=1, keepdims=True)
    owner_row = place_row[...] // shard_rows
    owner_column = place_column // shard_rows
    same = (owner_row == owner_column) & (down < across) & (down < count)
    rank = jnp.sum(same.astype(jnp.int32), axis=0, keepdims=True)
    slot = (owner_row ^ shard) * capacity + rank
    pick = ((slot == down) & (across < count)).astype(BF16)
    local = place_column - owner_column * shard_rows + 1
    tags = jnp.broadcast_to(local.astype(F32), (rows, META)).astype(BF16)
    normed = normed_rows(frames[...], gain[...])
    lead = first.shape[1] - META
    first[:, :lead] = jnp.dot(pick, normed[:, :lead], preferred_element_type=F32).astype(BF16)
    first[:, lead:] = jnp.dot(pick, tags, preferred_element_type=F32).astype(BF16)
    rest[...] = jnp.dot(pick, normed[:, lead:], preferred_element_type=F32).astype(BF16)


def make_slots(frames, gain, tile_pos, frame_count, shard, shard_rows, capacity, lead):
    rows, width = frames.shape
    scalars = jnp.stack([frame_count[0], shard.astype(jnp.int32)])
    return pl.pallas_call(
        functools.partial(slots_kernel, shard_rows=shard_rows, capacity=capacity),
        out_shape=(
            jax.ShapeDtypeStruct((rows, lead + META), BF16),
            jax.ShapeDtypeStruct((rows, width - lead), BF16),
        ),
        in_specs=[pl.BlockSpec(memory_space=pltpu.SMEM)]
        + [pl.BlockSpec(memory_space=pltpu.VMEM)] * 3,
        out_specs=(pl.BlockSpec(memory_space=pltpu.VMEM),) * 2,
        compiler_params=params(),
        cost_estimate=cost(2 * rows * rows * width, 4 * rows * width),
        name="frame_slots",
    )(scalars, frames, gain.reshape(1, width), tile_pos.reshape(1, rows))


def norm_kernel(rows, gain, out):
    out[...] = normed_rows(rows[...], gain[...])


def norm_text(text, gain):
    rows, width = text.shape
    step = 32
    return pl.pallas_call(
        norm_kernel,
        out_shape=jax.ShapeDtypeStruct((rows, width), BF16),
        grid=(rows // step,),
        in_specs=[
            pl.BlockSpec((step, width), lambda i: (i, 0)),
            pl.BlockSpec((1, width), lambda i: (0, 0)),
        ],
        out_specs=pl.BlockSpec((step, width), lambda i: (i, 0)),
        compiler_params=params(),
        cost_estimate=cost(4 * rows * width, 4 * rows * width),
        name="norm_text",
    )(text, gain.reshape(1, width))


def after(value, *earlier):
    return lax.optimization_barrier((value, earlier))[0]


def swap_slots(block, count, capacity):
    parts = [block[:capacity]]
    for d in range(1, count):
        pairs = [(i, i ^ d) for i in range(count)]
        parts.append(lax.ppermute(block[d * capacity : (d + 1) * capacity], "seq", pairs))
    return jnp.concatenate(parts, axis=0)


def hop_pairs(count, s, odd):
    links = range(odd, count - 1, 2)
    up = [(i, i + 1) for i in links if i >= s - 1]
    return up + [(i + 1, i) for i in links if i + 1 <= count - s]


def line_names(count):
    return ["own"] + [
        (s, odd) for s in range(1, count) for odd in (0, 1) if hop_pairs(count, s, odd)
    ]


def along_line(pieces, count):
    found = [{"own": piece} for piece in pieces]
    for s in range(1, count):
        for blocks in found:
            for odd in (0, 1):
                pairs = hop_pairs(count, s, odd)
                if pairs:
                    sent = blocks["own" if s == 1 else (s - 1, 1 - odd)]
                    blocks[(s, odd)] = lax.ppermute(sent, "vis", pairs)
    return [[blocks[name] for name in line_names(count)] for blocks in found]


def merge_kernel(*refs, blocks, rows, fresh):
    tags, incoming = refs[:blocks], refs[blocks : 2 * blocks]
    text, w_key, w_value = refs[2 * blocks : 2 * blocks + 3]
    merged, total, pick = refs[-3:]
    step = pl.program_id(0)
    slots = tags[0].shape[0]

    @pl.when(step == 0)
    def _():
        wanted = lax.broadcasted_iota(jnp.int32, (slots, rows), 1) + 1
        for b in range(blocks):
            place = tags[b][:, :1].astype(F32).astype(jnp.int32)
            pick[b * slots : (b + 1) * slots, :] = (place == wanted).astype(BF16)
        total[...] = jnp.zeros_like(total) if fresh else refs[-4][...]

    contract = (((0,), (0,)), ((), ()))
    found = jnp.concatenate([ref[...] for ref in incoming], axis=0)
    ones = jnp.ones((blocks * slots, META), BF16)
    covered = lax.dot_general(pick[...], ones, contract, preferred_element_type=F32)[:, :1]
    placed = lax.dot_general(pick[...], found, contract, preferred_element_type=F32)
    rows_here = jnp.where(covered > 0.5, placed.astype(BF16), text[...])
    merged[...] = rows_here
    half = w_key.shape[1]
    total[:, :half] += jnp.dot(rows_here, w_key[...], preferred_element_type=F32)
    total[:, half:] += jnp.dot(rows_here, w_value[...], preferred_element_type=F32)


def merge_chunk(tags, incoming, text, w_key, w_value, total, first, width):
    blocks, slots = len(tags), tags[0].shape[0]
    rows = text.shape[0]
    step = 512
    lead_step = first // step
    tag_column = width // META
    cols = w_key.shape[1]
    fresh = total is None
    return pl.pallas_call(
        functools.partial(merge_kernel, blocks=blocks, rows=rows, fresh=fresh),
        out_shape=(
            jax.ShapeDtypeStruct((rows, width), BF16),
            jax.ShapeDtypeStruct((rows, 2 * cols), F32),
        ),
        grid=(width // step,),
        in_specs=[pl.BlockSpec((slots, META), lambda i: (0, tag_column))] * blocks
        + [pl.BlockSpec((slots, step), lambda i: (0, i))] * blocks
        + [
            pl.BlockSpec((rows, step), lambda i: (0, i + lead_step)),
            pl.BlockSpec((step, cols), lambda i: (i + lead_step, 0)),
            pl.BlockSpec((step, cols), lambda i: (i + lead_step, 0)),
        ]
        + [pl.BlockSpec((rows, 2 * cols), lambda i: (0, 0))] * (not fresh),
        out_specs=(
            pl.BlockSpec((rows, step), lambda i: (0, i)),
            pl.BlockSpec((rows, 2 * cols), lambda i: (0, 0)),
        ),
        scratch_shapes=[pltpu.VMEM((blocks * slots, rows), BF16)],
        compiler_params=params(),
        cost_estimate=cost(
            2 * rows * width * (2 * cols + blocks * slots),
            2 * width * (blocks * slots + 2 * rows + 2 * cols),
        ),
        name="merge_rows",
    )(*tags, *incoming, text, w_key, w_value, *([] if fresh else [total]))


def query_kernel(*refs, parts):
    rows, (weights, bias, out) = refs[:parts], refs[parts:]
    total = bias[...]
    depth = rows[0].shape[1]
    for p in range(parts):
        total = total + jnp.dot(
            rows[p][...], weights[p * depth : (p + 1) * depth, :], preferred_element_type=F32
        )
    out[...] = total.astype(out.dtype)


def project_queries(parts, weights, first, earlier, dtype):
    rows, depth = parts[0].shape
    cols = weights.shape[1]
    taken = depth * len(parts)
    step = 512
    return pl.pallas_call(
        functools.partial(query_kernel, parts=len(parts)),
        out_shape=jax.ShapeDtypeStruct((rows, cols), dtype),
        grid=(cols // step,),
        in_specs=[pl.BlockSpec((rows, depth), lambda i: (0, 0))] * len(parts)
        + [
            pl.BlockSpec((taken, step), lambda i: (first // taken, i)),
            pl.BlockSpec((earlier.shape[0], step), lambda i: (0, i)),
        ],
        out_specs=pl.BlockSpec((rows, step), lambda i: (0, i)),
        compiler_params=params(),
        cost_estimate=cost(2 * rows * taken * cols, 2 * (rows + cols) * taken),
        name="queries",
    )(*parts, weights, earlier)


def attend_kernel(*refs, blocks, kv_heads, per_group, resume, finish):
    needed = refs[0]
    queries, docs_row, docs_column, places = refs[1], refs[2], refs[3], refs[4]
    keyvals = refs[5 : 5 + blocks]
    rest = refs[5 + blocks :]
    if resume:
        peak_in, total_in, sum_in = rest[:3]
        rest = rest[3:]
    if finish:
        out = rest[0]
        peak, total, summed = rest[1:]
    else:
        peak, total, summed = rest
    rows = queries.shape[0]
    heads = kv_heads * per_group
    scale = HEAD_DIM ** (-0.5)
    if resume:
        peak[...] = peak_in[...]
        total[...] = total_in[...]
        summed[...] = sum_in[...]
    else:
        peak[...] = jnp.full_like(peak, NEGATIVE)
        total[...] = jnp.zeros_like(total)
        summed[...] = jnp.zeros_like(summed)
    key_width = kv_heads * HEAD_DIM
    for b in range(blocks):

        @pl.when(needed[b] > 0)
        def _(b=b):
            distance = places[b]
            down = lax.broadcasted_iota(jnp.int32, (rows, rows), 0)
            across = lax.broadcasted_iota(jnp.int32, (rows, rows), 1)
            allowed = (down - distance <= across) & (docs_column[b] == docs_row[...])
            bias = jnp.where(allowed, 0.0, NEGATIVE)
            for g in range(kv_heads):
                keys = keyvals[b][:, g * HEAD_DIM : (g + 1) * HEAD_DIM]
                values = keyvals[b][:, key_width + g * HEAD_DIM : key_width + (g + 1) * HEAD_DIM]

                def one_head(j, _):
                    h = g * per_group + j
                    head_queries = queries[:, pl.ds(pl.multiple_of(h * HEAD_DIM, HEAD_DIM), HEAD_DIM)]
                    scores = lax.dot_general(
                        keys, head_queries, (((1,), (1,)), ((), ())), preferred_element_type=F32
                    )
                    scores = scores * scale + bias
                    old = peak[h]
                    new = jnp.maximum(old, jnp.max(scores, axis=0, keepdims=True))
                    raised = jnp.exp(scores - new)
                    factor = jnp.exp(old - new)
                    peak[h] = new
                    total[h] = total[h] * factor + jnp.sum(raised, axis=0, keepdims=True)
                    product = lax.dot_general(
                        values,
                        raised.astype(BF16),
                        (((0,), (0,)), ((), ())),
                        preferred_element_type=F32,
                    )
                    summed[h] = summed[h] * factor + product
                    return 0

                lax.fori_loop(0, per_group, one_head, 0, unroll=True)
    if finish:
        for h in range(heads):
            result = summed[h] / total[h]
            out[:, h * HEAD_DIM : (h + 1) * HEAD_DIM] = result.T.astype(BF16)


def attend(needed, queries, docs_row, docs_columns, places, keyvals, state, finish, kv_heads):
    rows, cols = queries.shape
    heads = cols // HEAD_DIM
    state_shapes = ((heads, 1, rows), (heads, 1, rows), (heads, HEAD_DIM, rows))
    vmem = pl.BlockSpec(memory_space=pltpu.VMEM)
    smem = pl.BlockSpec(memory_space=pltpu.SMEM)
    blocks = len(keyvals)
    out_shape = (
        jax.ShapeDtypeStruct((rows, cols), BF16)
        if finish
        else tuple(jax.ShapeDtypeStruct(s, F32) for s in state_shapes)
    )
    return pl.pallas_call(
        functools.partial(
            attend_kernel,
            blocks=blocks,
            kv_heads=kv_heads,
            per_group=heads // kv_heads,
            resume=state is not None,
            finish=finish,
        ),
        out_shape=out_shape,
        in_specs=[smem, vmem, vmem, vmem, smem] + [vmem] * (blocks + (3 if state else 0)),
        out_specs=vmem if finish else (vmem,) * 3,
        scratch_shapes=[pltpu.VMEM(s, F32) for s in state_shapes] if finish else [],
        compiler_params=params(),
        cost_estimate=cost(4 * rows * rows * cols * blocks, 4 * rows * cols),
        name="attend_rest" if finish else "attend_own",
    )(needed, queries, docs_row, docs_columns, places, *keyvals, *(state or ()))


def on_device(
    text, frames, tile_pos, frame_count, doc_ids, norm_gain, w_query, q_bias, w_key, w_value, v_bias
):
    seq_count = lax.axis_size("seq")
    vis_count = lax.axis_size("vis")
    shard = lax.axis_index("seq")
    rows, width = text.shape
    capacity = rows // (seq_count * vis_count)
    kv_heads = w_key.shape[1] // HEAD_DIM

    chunk = width // CHUNKS
    lead, rest = make_slots(
        frames, norm_gain, tile_pos, frame_count, shard, rows, capacity, chunk
    )
    lead = swap_slots(lead, seq_count, capacity)
    rest = swap_slots(after(rest, lead), seq_count, capacity)
    normed = norm_text(text, norm_gain)
    pieces = [lead] + [rest[:, i * chunk : (i + 1) * chunk] for i in range(CHUNKS - 1)]
    found = along_line(pieces, vis_count)
    merged, total = [], None
    cols = q_bias.shape[0]
    for c in range(CHUNKS):
        part, total = merge_chunk(
            found[0], found[c], normed, w_key, w_value, total, c * chunk, chunk
        )
        merged.append(part)
    queries = q_bias.reshape(1, cols)
    half = CHUNKS // 2
    for c in range(half):
        queries = project_queries([merged[c]], w_query, c * chunk, queries, F32)
    key_part = total[:, : w_key.shape[1]].astype(BF16)
    value_part = (total[:, w_key.shape[1] :] + v_bias).astype(BF16)
    keyval = jnp.concatenate([key_part, value_part], axis=1)

    core_swap = [(i, i ^ 1) for i in range(seq_count)]
    others = [(lax.ppermute(keyval, "seq", core_swap), shard ^ 1)]
    chips = seq_count // 2
    for mask in range(1, chips):
        pairs = [(c, c ^ mask) for c in range(chips) if 0 < (c ^ mask) - c <= chips // 2]
        pairs = [(2 * a + core, 2 * b + core) for a, b in pairs for core in (0, 1)]
        came = lax.ppermute(keyval, "seq", pairs)
        others.append((came, shard ^ (2 * mask)))
        others.append((lax.ppermute(came, "seq", core_swap), shard ^ (2 * mask + 1)))

    queries = project_queries(merged[half:], w_query, half * chunk, queries, BF16)
    docs = doc_ids.reshape(seq_count, rows)
    docs_row = lax.dynamic_slice_in_dim(docs, shard, 1)
    docs_own = docs_row.reshape(1, rows, 1)
    one = jnp.ones((1,), jnp.int32)
    state = attend(
        one, queries, docs_row, docs_own, 0 * one, [keyval], None, False, kv_heads
    )
    origins = jnp.stack([origin for _, origin in others]).astype(jnp.int32)
    other_docs = docs[origins]
    needed = (origins < shard) & (other_docs[:, -1] >= docs_row[0, 0])
    return attend(
        needed.astype(jnp.int32),
        queries,
        docs_row,
        other_docs.reshape(-1, rows, 1),
        (shard - origins).astype(jnp.int32) * rows,
        [entry for entry, _ in others],
        state,
        True,
        kv_heads,
    )


def solution(mesh):
    in_specs = (
        P("seq", None),
        P(("seq", "vis"), None),
        P(("seq", "vis")),
        P(("seq", "vis")),
        P(),
        P(),
        P(None, "vis"),
        P("vis"),
        P(None, "vis"),
        P(None, "vis"),
        P("vis"),
    )
    return jax.shard_map(
        on_device, mesh=mesh, in_specs=in_specs, out_specs=P("seq", "vis"), check_vma=False
    )
```

```python
import functools

import jax
import jax.numpy as jnp
from jax import lax
from jax.experimental import pallas as pl
from jax.experimental.pallas import tpu as pltpu
from jax.sharding import PartitionSpec as P

HEAD_DIM = 128
META = 128
CHUNKS = 4
EPSILON = 1e-06
NEGATIVE = -1e30
LOG2_E = 1.4426950408889634
VMEM_LIMIT = 48 * 1024 * 1024
F32 = jnp.float32
BF16 = jnp.bfloat16


def params(limit=VMEM_LIMIT):
    return pltpu.CompilerParams(vmem_limit_bytes=limit)


def cost(flops, moved):
    return pl.CostEstimate(flops=int(flops), bytes_accessed=int(moved), transcendentals=0)


def normed_rows(rows, gain):
    widened = rows.astype(F32)
    mean_square = jnp.mean(widened * widened, axis=1, keepdims=True)
    return (widened * lax.rsqrt(mean_square + EPSILON) * gain).astype(BF16)


def slots_kernel(scalars, frames, gain, place_row, out, *, shard_rows, capacity):
    count, shard = scalars[0], scalars[1]
    rows, width = frames.shape
    across = lax.broadcasted_iota(jnp.int32, (rows, rows), 1)
    down = lax.broadcasted_iota(jnp.int32, (rows, rows), 0)
    places = jnp.broadcast_to(place_row[...], (rows, rows))
    place_column = jnp.sum(jnp.where(down == across, places, 0), axis=1, keepdims=True)
    owner_row = place_row[...] // shard_rows
    owner_column = place_column // shard_rows
    same = (owner_row == owner_column) & (down < across) & (down < count)
    rank = jnp.sum(same.astype(jnp.int32), axis=0, keepdims=True)
    slot = (owner_row ^ shard) * capacity + rank
    pick = ((slot == down) & (across < count)).astype(BF16)
    local = place_column - owner_column * shard_rows + 1
    tags = jnp.broadcast_to(local.astype(F32), (rows, META)).astype(BF16)
    normed = normed_rows(frames[...], gain[...])
    lead = (out.shape[1] - META) // CHUNKS
    out[:, :lead] = jnp.dot(pick, normed[:, :lead], preferred_element_type=F32).astype(BF16)
    out[:, lead : lead + META] = jnp.dot(pick, tags, preferred_element_type=F32).astype(BF16)
    out[:, lead + META :] = jnp.dot(pick, normed[:, lead:], preferred_element_type=F32).astype(BF16)


def make_slots(frames, gain, tile_pos, frame_count, shard, shard_rows, capacity):
    rows, width = frames.shape
    scalars = jnp.stack([frame_count[0], shard.astype(jnp.int32)])
    return pl.pallas_call(
        functools.partial(slots_kernel, shard_rows=shard_rows, capacity=capacity),
        out_shape=jax.ShapeDtypeStruct((rows, width + META), BF16),
        in_specs=[pl.BlockSpec(memory_space=pltpu.SMEM)]
        + [pl.BlockSpec(memory_space=pltpu.VMEM)] * 3,
        out_specs=pl.BlockSpec(memory_space=pltpu.VMEM),
        compiler_params=params(),
        cost_estimate=cost(2 * rows * rows * width, 4 * rows * width),
        name="frame_slots",
    )(scalars, frames, gain.reshape(1, width), tile_pos.reshape(1, rows))


def scale_kernel(rows, out):
    widened = rows[...].astype(F32)
    mean_square = jnp.mean(widened * widened, axis=1, keepdims=True)
    out[...] = jnp.broadcast_to(lax.rsqrt(mean_square + EPSILON), out.shape)


def text_scale(text):
    rows, width = text.shape
    step = 64
    return pl.pallas_call(
        scale_kernel,
        out_shape=jax.ShapeDtypeStruct((rows, META), F32),
        grid=(rows // step,),
        in_specs=[pl.BlockSpec((step, width), lambda i: (i, 0))],
        out_specs=pl.BlockSpec((step, META), lambda i: (i, 0)),
        compiler_params=params(),
        cost_estimate=cost(3 * rows * width, 2 * rows * width),
        name="text_scale",
    )(text)


def assemble_kernel(*refs, parts):
    at = 0
    for out in refs[parts:]:
        end = at + out.shape[1]
        found = [ref[:, at:end].astype(F32) for ref in refs[:parts]]
        out[...] = jnp.concatenate(found, axis=0).astype(BF16)
        at = end


def assemble(parts, widths):
    rows = sum(part.shape[0] for part in parts)
    if parts[0].shape[0] % 8:
        whole = jnp.concatenate(parts)
        cuts = [sum(widths[:i]) for i in range(len(widths) + 1)]
        return [whole[:, a:b] for a, b in zip(cuts, cuts[1:])]
    vmem = pl.BlockSpec(memory_space=pltpu.VMEM)
    return pl.pallas_call(
        functools.partial(assemble_kernel, parts=len(parts)),
        out_shape=[jax.ShapeDtypeStruct((rows, width), BF16) for width in widths],
        in_specs=[vmem] * len(parts),
        out_specs=[vmem] * len(widths),
        compiler_params=params(),
        cost_estimate=cost(rows * sum(widths), 4 * rows * sum(widths)),
        name="assemble",
    )(*parts)


def after(value, *earlier):
    return lax.optimization_barrier((value, earlier))[0]


def swap_slots(block, count, capacity):
    parts = [block[:capacity]]
    for d in range(1, count):
        sent = block[d * capacity : (d + 1) * capacity]
        parts.append(lax.ppermute(sent, "seq", [(i, i ^ d) for i in range(count)]))
    return parts


def hop_pairs(count, s, odd):
    links = range(odd, count - 1, 2)
    up = [(i, i + 1) for i in links if i >= s - 1]
    return up + [(i + 1, i) for i in links if i + 1 <= count - s]


def merge_kernel(*refs, blocks, rows, fresh, finish):
    tags, incoming = refs[:blocks], refs[blocks : 2 * blocks]
    text, scale, gain, w_key, w_value = refs[2 * blocks : 2 * blocks + 5]
    merged, keyval = refs[-5], refs[-4]
    total, pick, covered = refs[-3:]
    step = pl.program_id(0)
    slots = tags[0].shape[0]
    half = w_key.shape[1]

    @pl.when(step == 0)
    def _():
        places = jnp.concatenate([ref[...] for ref in tags], axis=0).astype(F32).T[:1, :]
        wanted = lax.broadcasted_iota(jnp.int32, (rows, blocks * slots), 0) + 1
        chosen = (places.astype(jnp.int32) == wanted).astype(F32)
        pick[...] = chosen.astype(BF16)
        covered[...] = jnp.broadcast_to(jnp.sum(chosen, axis=1, keepdims=True), covered.shape)
        total[...] = jnp.zeros_like(total) if fresh else refs[2 * blocks + 5][...]

    found = jnp.concatenate([ref[...] for ref in incoming], axis=0)
    placed = jnp.dot(pick[...], found, preferred_element_type=F32)
    normed = text[...].astype(F32) * scale[:, :1] * gain[...]
    rows_here = jnp.where(covered[:, :1] > 0.5, placed, normed).astype(BF16)
    merged[...] = rows_here
    total[:, :half] += jnp.dot(rows_here, w_key[...], preferred_element_type=F32)
    total[:, half:] += jnp.dot(rows_here, w_value[...], preferred_element_type=F32)

    @pl.when(step == pl.num_programs(0) - 1)
    def _():
        if finish:
            v_bias = refs[2 * blocks + 6]
            keyval[:, :half] = total[:, :half].astype(BF16)
            keyval[:, half:] = (total[:, half:] + v_bias[...]).astype(BF16)
        else:
            keyval[...] = total[...]


def merge_chunk(
    tags, incoming, text, scale, gain, w_key, w_value, total, first, width, v_bias, earlier
):
    blocks, slots = len(tags), tags[0].shape[0]
    rows = text.shape[0]
    step = 1024
    lead_step = first // step
    tag_column = width // META
    cols = w_key.shape[1]
    fresh, finish = total is None, v_bias is not None
    whole = pl.BlockSpec((rows, 2 * cols), lambda i: (0, 0))
    extra = [] if fresh else [total]
    extra_specs = [] if fresh else [whole]
    if finish:
        extra.append(v_bias.reshape(1, cols))
        extra_specs.append(pl.BlockSpec((1, cols), lambda i: (0, 0)))
    extra += earlier
    extra_specs += [pl.BlockSpec(memory_space=pl.ANY)] * len(earlier)
    return pl.pallas_call(
        functools.partial(merge_kernel, blocks=blocks, rows=rows, fresh=fresh, finish=finish),
        out_shape=(
            jax.ShapeDtypeStruct((rows, width), BF16),
            jax.ShapeDtypeStruct((rows, 2 * cols), BF16 if finish else F32),
        ),
        grid=(width // step,),
        in_specs=[pl.BlockSpec((slots, META), lambda i: (0, tag_column))] * blocks
        + [pl.BlockSpec((slots, step), lambda i: (0, i))] * blocks
        + [
            pl.BlockSpec((rows, step), lambda i: (0, i + lead_step)),
            pl.BlockSpec((rows, META), lambda i: (0, 0)),
            pl.BlockSpec((1, step), lambda i: (0, i + lead_step)),
            pl.BlockSpec((step, cols), lambda i: (i + lead_step, 0)),
            pl.BlockSpec((step, cols), lambda i: (i + lead_step, 0)),
        ]
        + extra_specs,
        out_specs=(pl.BlockSpec((rows, step), lambda i: (0, i)), whole),
        scratch_shapes=[
            pltpu.VMEM((rows, 2 * cols), F32),
            pltpu.VMEM((rows, blocks * slots), BF16),
            pltpu.VMEM((rows, META), F32),
        ],
        compiler_params=params(),
        cost_estimate=cost(
            2 * rows * width * (2 * cols + blocks * slots),
            2 * width * (blocks * slots + 2 * rows + 2 * cols),
        ),
        name="merge_rows",
    )(*tags, *incoming, text, scale, gain.reshape(1, -1), w_key, w_value, *extra)


def query_kernel(*refs, parts, finish):
    rows, (weights, bias, out) = refs[:parts], refs[parts:]
    total = bias[...]
    depth = rows[0].shape[1]
    for p in range(parts):
        total = total + jnp.dot(
            rows[p][...], weights[p * depth : (p + 1) * depth, :], preferred_element_type=F32
        )
    if finish:
        count = total.shape[0]
        for j in range(total.shape[1] // HEAD_DIM):
            head = total[:, j * HEAD_DIM : (j + 1) * HEAD_DIM]
            out[0, :, j * count : (j + 1) * count] = head.T.astype(BF16)
    else:
        out[...] = total


def project_queries(parts, weights, first, earlier, groups):
    rows, depth = parts[0].shape
    cols = weights.shape[1]
    taken = depth * len(parts)
    step = 512
    out_shape = jax.ShapeDtypeStruct((rows, cols), F32)
    out_spec = pl.BlockSpec((rows, step), lambda i: (0, i))
    if groups:
        wide = cols // groups // HEAD_DIM * rows
        share = cols // groups // step
        out_shape = jax.ShapeDtypeStruct((groups, HEAD_DIM, wide), BF16)
        out_spec = pl.BlockSpec((1, HEAD_DIM, wide // share), lambda i: (i // share, 0, i % share))
    return pl.pallas_call(
        functools.partial(query_kernel, parts=len(parts), finish=groups > 0),
        out_shape=out_shape,
        grid=(cols // step,),
        in_specs=[pl.BlockSpec((rows, depth), lambda i: (0, 0))] * len(parts)
        + [
            pl.BlockSpec((taken, step), lambda i: (first // taken, i)),
            pl.BlockSpec((earlier.shape[0], step), lambda i: (0, i)),
        ],
        out_specs=out_spec,
        compiler_params=params(),
        cost_estimate=cost(2 * rows * taken * cols, 2 * (rows + cols) * taken),
        name="queries",
    )(*parts, weights, earlier)


def attend_kernel(*refs, blocks, kv_heads, resume, finish):
    needed, queries, docs_row, docs_column, places = refs[:5]
    keyvals = refs[5 : 5 + blocks]
    rest = refs[5 + blocks :]
    earlier, rest = (rest[:3], rest[3:]) if resume else (None, rest)
    out, (peak, total, summed) = (rest[0], rest[1:]) if finish else (None, rest)
    rows = docs_row.shape[1]
    wide = queries.shape[2]
    span = 8 * rows
    scale = HEAD_DIM ** (-0.5) * LOG2_E
    if resume:
        peak[...] = earlier[0][...]
        total[...] = earlier[1][...]
        summed[...] = earlier[2][...]
    else:
        peak[...] = jnp.full_like(peak, NEGATIVE)
        total[...] = jnp.zeros_like(total)
        summed[...] = jnp.zeros_like(summed)
    key_width = kv_heads * HEAD_DIM

    def one_block(b):
        down = lax.broadcasted_iota(jnp.int32, (rows, rows), 0)
        across = lax.broadcasted_iota(jnp.int32, (rows, rows), 1)
        allowed = (down - places[b] <= across) & (docs_column[b] == docs_row[...])
        bias = jnp.where(allowed, 0.0, NEGATIVE)
        bias = jnp.concatenate([bias] * (span // rows), axis=1)
        for g in range(kv_heads):
            keys = keyvals[b][:, g * HEAD_DIM : (g + 1) * HEAD_DIM]
            values = keyvals[b][:, key_width + g * HEAD_DIM : key_width + (g + 1) * HEAD_DIM].T
            for at in range(0, wide, span):
                part = slice(at, at + span)
                scores = jnp.dot(keys, queries[g, :, part], preferred_element_type=F32)
                scores = scores * scale + bias
                old = peak[g, :, part]
                new = jnp.maximum(old, jnp.max(scores, axis=0, keepdims=True))
                raised = jnp.exp2(scores - new)
                factor = jnp.exp2(old - new)
                peak[g, :, part] = new
                total[g, :, part] = total[g, :, part] * factor + jnp.sum(
                    raised, axis=0, keepdims=True
                )
                product = jnp.dot(values, raised.astype(BF16), preferred_element_type=F32)
                summed[g, :, part] = summed[g, :, part] * factor + product

    for b in range(blocks):
        pl.when(needed[b] > 0)(functools.partial(one_block, b))
    if finish:
        for g in range(kv_heads):
            for j in range(wide // rows):
                part = slice(j * rows, (j + 1) * rows)
                result = (summed[g, :, part] * (1.0 / total[g, :, part])).T
                at = (g * (wide // rows) + j) * HEAD_DIM
                out[:, at : at + HEAD_DIM] = result.astype(BF16)


def attend(needed, queries, docs_row, docs_columns, places, keyvals, state, finish, kv_heads):
    wide = queries.shape[2]
    rows = docs_row.shape[1]
    cols = kv_heads * wide // rows * HEAD_DIM
    state_shapes = ((kv_heads, 1, wide), (kv_heads, 1, wide), (kv_heads, HEAD_DIM, wide))
    vmem = pl.BlockSpec(memory_space=pltpu.VMEM)
    smem = pl.BlockSpec(memory_space=pltpu.SMEM)
    blocks = len(keyvals)
    out_shape = (
        jax.ShapeDtypeStruct((rows, cols), BF16)
        if finish
        else tuple(jax.ShapeDtypeStruct(s, F32) for s in state_shapes)
    )
    return pl.pallas_call(
        functools.partial(
            attend_kernel,
            blocks=blocks,
            kv_heads=kv_heads,
            resume=state is not None,
            finish=finish,
        ),
        out_shape=out_shape,
        in_specs=[smem, vmem, vmem, vmem, smem] + [vmem] * (blocks + (3 if state else 0)),
        out_specs=vmem if finish else (vmem,) * 3,
        scratch_shapes=[pltpu.VMEM(s, F32) for s in state_shapes] if finish else [],
        compiler_params=params(),
        cost_estimate=cost(4 * rows * rows * cols * blocks, 4 * rows * cols),
        name="attend_rest" if finish else "attend_own",
    )(needed, queries, docs_row, docs_columns, places, *keyvals, *(state or ()))


def on_device(
    text, frames, tile_pos, frame_count, doc_ids, norm_gain, w_query, q_bias, w_key, w_value, v_bias
):
    seq_count = lax.axis_size("seq")
    vis_count = lax.axis_size("vis")
    shard = lax.axis_index("seq")
    rows, width = text.shape
    capacity = rows // (seq_count * vis_count)
    kv_heads = w_key.shape[1] // HEAD_DIM

    chunk = width // CHUNKS
    slots = make_slots(frames, norm_gain, tile_pos, frame_count, shard, rows, capacity)
    parts = swap_slots(slots, seq_count, capacity)
    pieces = assemble(parts, [chunk + META] + [chunk] * (CHUNKS - 1))
    scale = text_scale(after(text, pieces[0]))
    found = [{} for _ in pieces]
    merged, sums = [], {"total": None, "queries": q_bias.reshape(1, -1)}

    def hop(c, s, *earlier):
        for odd in (0, 1):
            pairs = hop_pairs(vis_count, s, odd)
            if pairs:
                sent = pieces[c] if s == 1 else found[c][(s - 1, 1 - odd)]
                if earlier:
                    sent = after(sent, *earlier)
                found[c][(s, odd)] = lax.ppermute(sent, "vis", pairs)
        return [found[c][(s, odd)] for odd in (0, 1) if (s, odd) in found[c]]

    def merge(c, *earlier):
        part, sums["total"] = merge_chunk(
            [pieces[0], *found[0].values()],
            [pieces[c], *found[c].values()],
            text,
            scale,
            norm_gain,
            w_key,
            w_value,
            sums["total"],
            c * chunk,
            chunk,
            v_bias if c == CHUNKS - 1 else None,
            list(earlier),
        )
        merged.append(part)

    def query(c):
        sums["queries"] = project_queries([merged[c]], w_query, c * chunk, sums["queries"], 0)

    for s in range(1, vis_count):
        for c in range(CHUNKS):
            hop(c, s)
    for c in range(CHUNKS):
        if c == 2:
            query(0)
            query(1)
        merge(c, *([sums["queries"]] if c == 2 else []))
    keyval = sums["total"]

    half = CHUNKS // 2
    queries = project_queries(
        merged[half:], w_query, half * chunk, sums["queries"], kv_heads
    )

    chips = seq_count // 2
    near, others = [(keyval, shard)], []
    for mask in range(1, chips):
        pairs = [(c, c ^ mask) for c in range(chips) if 0 < (c ^ mask) - c <= chips // 2]
        pairs = [(2 * a + core, 2 * b + core) for a, b in pairs for core in (0, 1)]
        near.append((lax.ppermute(keyval, "seq", pairs), shard ^ (2 * mask)))
    docs = doc_ids.reshape(seq_count, rows)
    docs_row = lax.dynamic_slice_in_dim(docs, shard, 1)
    docs_own = docs_row.reshape(1, rows, 1)
    one = jnp.ones((1,), jnp.int32)
    state = attend(
        one, queries, docs_row, docs_own, 0 * one, [keyval], None, False, kv_heads
    )
    core_swap = [(i, i ^ 1) for i in range(seq_count)]
    for held, origin in near:
        others.append((lax.ppermute(after(held, state[0]), "seq", core_swap), origin ^ 1))
    others += near[1:]

    origins = jnp.stack([origin for _, origin in others]).astype(jnp.int32)
    other_docs = docs[origins]
    needed = (origins < shard) & (other_docs[:, -1] >= docs_row[0, 0])
    return attend(
        needed.astype(jnp.int32),
        queries,
        docs_row,
        other_docs.reshape(-1, rows, 1),
        (shard - origins).astype(jnp.int32) * rows,
        [entry for entry, _ in others],
        state,
        True,
        kv_heads,
    )


def solution(mesh):
    in_specs = (
        P("seq", None),
        P(("seq", "vis"), None),
        P(("seq", "vis")),
        P(("seq", "vis")),
        P(),
        P(),
        P(None, "vis"),
        P("vis"),
        P(None, "vis"),
        P(None, "vis"),
        P("vis"),
    )
    return jax.shard_map(
        on_device, mesh=mesh, in_specs=in_specs, out_specs=P("seq", "vis"), check_vma=False
    )
```

```python
import functools

import jax
import jax.numpy as jnp
from jax import lax
from jax.experimental import pallas as pl
from jax.experimental.pallas import tpu as pltpu
from jax.sharding import PartitionSpec as P

HEAD_DIM = 128
META = 128
CHUNKS = 4
EPSILON = 1e-06
NEGATIVE = -1e30
LOG2_E = 1.4426950408889634
VMEM_LIMIT = 48 * 1024 * 1024
F32 = jnp.float32
BF16 = jnp.bfloat16


def params(limit=VMEM_LIMIT):
    return pltpu.CompilerParams(vmem_limit_bytes=limit)


def cost(flops, moved):
    return pl.CostEstimate(flops=int(flops), bytes_accessed=int(moved), transcendentals=0)


def normed_rows(rows, gain):
    widened = rows.astype(F32)
    mean_square = jnp.mean(widened * widened, axis=1, keepdims=True)
    return (widened * lax.rsqrt(mean_square + EPSILON) * gain).astype(BF16)


def slots_kernel(
    scalars, frames_in, gain_in, places_in, out, frames, gain, place_row, sems, *, shard_rows, capacity
):
    fetches = [
        pltpu.make_async_copy(source, target, sems.at[i])
        for i, (source, target) in enumerate(
            ((places_in, place_row), (gain_in, gain), (frames_in, frames))
        )
    ]
    for fetch in fetches:
        fetch.start()
    for fetch in fetches:
        fetch.wait()
    count, shard = scalars[0], scalars[1]
    rows, width = frames.shape
    across = lax.broadcasted_iota(jnp.int32, (rows, rows), 1)
    down = lax.broadcasted_iota(jnp.int32, (rows, rows), 0)
    places = jnp.broadcast_to(place_row[...], (rows, rows))
    place_column = jnp.sum(jnp.where(down == across, places, 0), axis=1, keepdims=True)
    owner_row = place_row[...] // shard_rows
    owner_column = place_column // shard_rows
    same = (owner_row == owner_column) & (down < across) & (down < count)
    rank = jnp.sum(same.astype(jnp.int32), axis=0, keepdims=True)
    slot = (owner_row ^ shard) * capacity + rank
    pick = ((slot == down) & (across < count)).astype(BF16)
    local = place_column - owner_column * shard_rows + 1
    tags = jnp.broadcast_to(local.astype(F32), (rows, META)).astype(BF16)
    normed = normed_rows(frames[...], gain[...])
    lead = (out.shape[1] - META) // CHUNKS
    out[:, :lead] = jnp.dot(pick, normed[:, :lead], preferred_element_type=F32).astype(BF16)
    out[:, lead : lead + META] = jnp.dot(pick, tags, preferred_element_type=F32).astype(BF16)
    out[:, lead + META :] = jnp.dot(pick, normed[:, lead:], preferred_element_type=F32).astype(BF16)


def make_slots(frames, gain, tile_pos, frame_count, shard, shard_rows, capacity):
    rows, width = frames.shape
    scalars = jnp.stack([frame_count[0], shard.astype(jnp.int32)])
    return pl.pallas_call(
        functools.partial(slots_kernel, shard_rows=shard_rows, capacity=capacity),
        out_shape=jax.ShapeDtypeStruct((rows, width + META), BF16),
        in_specs=[pl.BlockSpec(memory_space=pltpu.SMEM)]
        + [pl.BlockSpec(memory_space=pl.ANY)] * 3,
        out_specs=pl.BlockSpec(memory_space=pltpu.VMEM),
        scratch_shapes=[
            pltpu.VMEM((rows, width), BF16),
            pltpu.VMEM((1, width), F32),
            pltpu.VMEM((1, rows), jnp.int32),
            pltpu.SemaphoreType.DMA((3,)),
        ],
        compiler_params=params(),
        cost_estimate=cost(2 * rows * rows * width, 4 * rows * width),
        name="frame_slots",
    )(scalars, frames, gain.reshape(1, width), tile_pos.reshape(1, rows))


def scale_kernel(rows, out):
    widened = rows[...].astype(F32)
    mean_square = jnp.mean(widened * widened, axis=1, keepdims=True)
    out[...] = jnp.broadcast_to(lax.rsqrt(mean_square + EPSILON), out.shape)


def text_scale(text):
    rows, width = text.shape
    step = 64
    return pl.pallas_call(
        scale_kernel,
        out_shape=jax.ShapeDtypeStruct((rows, META), F32),
        grid=(rows // step,),
        in_specs=[pl.BlockSpec((step, width), lambda i: (i, 0))],
        out_specs=pl.BlockSpec((step, META), lambda i: (i, 0)),
        compiler_params=params(),
        cost_estimate=cost(3 * rows * width, 2 * rows * width),
        name="text_scale",
    )(text)


def assemble_kernel(*refs, parts):
    at = 0
    for out in refs[parts:]:
        end = at + out.shape[1]
        found = [ref[:, at:end].astype(F32) for ref in refs[:parts]]
        out[...] = jnp.concatenate(found, axis=0).astype(BF16)
        at = end


def assemble(parts, widths):
    rows = sum(part.shape[0] for part in parts)
    if parts[0].shape[0] % 8:
        whole = jnp.concatenate(parts)
        cuts = [sum(widths[:i]) for i in range(len(widths) + 1)]
        return [whole[:, a:b] for a, b in zip(cuts, cuts[1:])]
    vmem = pl.BlockSpec(memory_space=pltpu.VMEM)
    return pl.pallas_call(
        functools.partial(assemble_kernel, parts=len(parts)),
        out_shape=[jax.ShapeDtypeStruct((rows, width), BF16) for width in widths],
        in_specs=[vmem] * len(parts),
        out_specs=[vmem] * len(widths),
        compiler_params=params(),
        cost_estimate=cost(rows * sum(widths), 4 * rows * sum(widths)),
        name="assemble",
    )(*parts)


def after(value, *earlier):
    return lax.optimization_barrier((value, earlier))[0]


def swap_slots(block, count, capacity):
    parts = [block[:capacity]]
    for d in range(1, count):
        sent = block[d * capacity : (d + 1) * capacity]
        parts.append(lax.ppermute(sent, "seq", [(i, i ^ d) for i in range(count)]))
    return parts


def hop_pairs(count, s, odd):
    links = range(odd, count - 1, 2)
    up = [(i, i + 1) for i in links if i >= s - 1]
    return up + [(i + 1, i) for i in links if i + 1 <= count - s]


def merge_kernel(*refs, blocks, rows, fresh, finish):
    tags, incoming = refs[:blocks], refs[blocks : 2 * blocks]
    text, scale, gain, w_key, w_value = refs[2 * blocks : 2 * blocks + 5]
    merged, keyval = refs[-5], refs[-4]
    total, pick, covered = refs[-3:]
    step = pl.program_id(0)
    slots = tags[0].shape[0]
    half = w_key.shape[1]

    @pl.when(step == 0)
    def _():
        places = jnp.concatenate([ref[...] for ref in tags], axis=0).astype(F32).T[:1, :]
        wanted = lax.broadcasted_iota(jnp.int32, (rows, blocks * slots), 0) + 1
        chosen = (places.astype(jnp.int32) == wanted).astype(F32)
        pick[...] = chosen.astype(BF16)
        covered[...] = jnp.broadcast_to(jnp.sum(chosen, axis=1, keepdims=True), covered.shape)
        total[...] = jnp.zeros_like(total) if fresh else refs[2 * blocks + 5][...]

    found = jnp.concatenate([ref[...] for ref in incoming], axis=0)
    placed = jnp.dot(pick[...], found, preferred_element_type=F32)
    normed = text[...].astype(F32) * scale[:, :1] * gain[...]
    rows_here = jnp.where(covered[:, :1] > 0.5, placed, normed).astype(BF16)
    merged[...] = rows_here
    total[:, :half] += jnp.dot(rows_here, w_key[...], preferred_element_type=F32)
    total[:, half:] += jnp.dot(rows_here, w_value[...], preferred_element_type=F32)

    @pl.when(step == pl.num_programs(0) - 1)
    def _():
        if finish:
            v_bias = refs[2 * blocks + 6]
            keyval[:, :half] = total[:, :half].astype(BF16)
            keyval[:, half:] = (total[:, half:] + v_bias[...]).astype(BF16)
        else:
            keyval[...] = total[...]


def merge_chunk(
    tags, incoming, text, scale, gain, w_key, w_value, total, first, width, v_bias, earlier
):
    blocks, slots = len(tags), tags[0].shape[0]
    rows = text.shape[0]
    step = 1024
    lead_step = first // step
    tag_column = width // META
    cols = w_key.shape[1]
    fresh, finish = total is None, v_bias is not None
    whole = pl.BlockSpec((rows, 2 * cols), lambda i: (0, 0))
    extra = [] if fresh else [total]
    extra_specs = [] if fresh else [whole]
    if finish:
        extra.append(v_bias.reshape(1, cols))
        extra_specs.append(pl.BlockSpec((1, cols), lambda i: (0, 0)))
    extra += earlier
    extra_specs += [pl.BlockSpec(memory_space=pl.ANY)] * len(earlier)
    return pl.pallas_call(
        functools.partial(merge_kernel, blocks=blocks, rows=rows, fresh=fresh, finish=finish),
        out_shape=(
            jax.ShapeDtypeStruct((rows, width), BF16),
            jax.ShapeDtypeStruct((rows, 2 * cols), BF16 if finish else F32),
        ),
        grid=(width // step,),
        in_specs=[pl.BlockSpec((slots, META), lambda i: (0, tag_column))] * blocks
        + [pl.BlockSpec((slots, step), lambda i: (0, i))] * blocks
        + [
            pl.BlockSpec((rows, step), lambda i: (0, i + lead_step)),
            pl.BlockSpec((rows, META), lambda i: (0, 0)),
            pl.BlockSpec((1, step), lambda i: (0, i + lead_step)),
            pl.BlockSpec((step, cols), lambda i: (i + lead_step, 0)),
            pl.BlockSpec((step, cols), lambda i: (i + lead_step, 0)),
        ]
        + extra_specs,
        out_specs=(pl.BlockSpec((rows, step), lambda i: (0, i)), whole),
        scratch_shapes=[
            pltpu.VMEM((rows, 2 * cols), F32),
            pltpu.VMEM((rows, blocks * slots), BF16),
            pltpu.VMEM((rows, META), F32),
        ],
        compiler_params=params(),
        cost_estimate=cost(
            2 * rows * width * (2 * cols + blocks * slots),
            2 * width * (blocks * slots + 2 * rows + 2 * cols),
        ),
        name="merge_rows",
    )(*tags, *incoming, text, scale, gain.reshape(1, -1), w_key, w_value, *extra)


def query_kernel(*refs, parts, finish):
    rows, (weights, bias, out) = refs[:parts], refs[parts:]
    total = bias[...]
    depth = rows[0].shape[1]
    for p in range(parts):
        total = total + jnp.dot(
            rows[p][...], weights[p * depth : (p + 1) * depth, :], preferred_element_type=F32
        )
    if finish:
        count = total.shape[0]
        for j in range(total.shape[1] // HEAD_DIM):
            head = total[:, j * HEAD_DIM : (j + 1) * HEAD_DIM]
            out[0, :, j * count : (j + 1) * count] = head.T.astype(BF16)
    else:
        out[...] = total


def project_queries(parts, weights, first, earlier, groups):
    rows, depth = parts[0].shape
    cols = weights.shape[1]
    taken = depth * len(parts)
    step = 512
    out_shape = jax.ShapeDtypeStruct((rows, cols), F32)
    out_spec = pl.BlockSpec((rows, step), lambda i: (0, i))
    if groups:
        wide = cols // groups // HEAD_DIM * rows
        share = cols // groups // step
        out_shape = jax.ShapeDtypeStruct((groups, HEAD_DIM, wide), BF16)
        out_spec = pl.BlockSpec((1, HEAD_DIM, wide // share), lambda i: (i // share, 0, i % share))
    return pl.pallas_call(
        functools.partial(query_kernel, parts=len(parts), finish=groups > 0),
        out_shape=out_shape,
        grid=(cols // step,),
        in_specs=[pl.BlockSpec((rows, depth), lambda i: (0, 0))] * len(parts)
        + [
            pl.BlockSpec((taken, step), lambda i: (first // taken, i)),
            pl.BlockSpec((earlier.shape[0], step), lambda i: (0, i)),
        ],
        out_specs=out_spec,
        compiler_params=params(),
        cost_estimate=cost(2 * rows * taken * cols, 2 * (rows + cols) * taken),
        name="queries",
    )(*parts, weights, earlier)


def attend_kernel(*refs, blocks, kv_heads, resume, finish):
    needed, queries, docs_row, docs_column, places = refs[:5]
    keyvals = refs[5 : 5 + blocks]
    rest = refs[5 + blocks :]
    earlier, rest = (rest[:3], rest[3:]) if resume else (None, rest)
    out, (peak, total, summed) = (rest[0], rest[1:]) if finish else (None, rest)
    rows = docs_row.shape[1]
    wide = queries.shape[2]
    span = 8 * rows
    scale = HEAD_DIM ** (-0.5) * LOG2_E
    if resume:
        peak[...] = earlier[0][...]
        total[...] = earlier[1][...]
        summed[...] = earlier[2][...]
    else:
        peak[...] = jnp.full_like(peak, NEGATIVE)
        total[...] = jnp.zeros_like(total)
        summed[...] = jnp.zeros_like(summed)
    key_width = kv_heads * HEAD_DIM

    def one_block(b):
        down = lax.broadcasted_iota(jnp.int32, (rows, rows), 0)
        across = lax.broadcasted_iota(jnp.int32, (rows, rows), 1)
        allowed = (down - places[b] <= across) & (docs_column[b] == docs_row[...])
        bias = jnp.where(allowed, 0.0, NEGATIVE)
        bias = jnp.concatenate([bias] * (span // rows), axis=1)
        for g in range(kv_heads):
            keys = keyvals[b][:, g * HEAD_DIM : (g + 1) * HEAD_DIM]
            values = keyvals[b][:, key_width + g * HEAD_DIM : key_width + (g + 1) * HEAD_DIM].T
            for at in range(0, wide, span):
                part = slice(at, at + span)
                scores = jnp.dot(keys, queries[g, :, part], preferred_element_type=F32)
                scores = scores * scale + bias
                old = peak[g, :, part]
                new = jnp.maximum(old, jnp.max(scores, axis=0, keepdims=True))
                raised = jnp.exp2(scores - new)
                factor = jnp.exp2(old - new)
                peak[g, :, part] = new
                total[g, :, part] = total[g, :, part] * factor + jnp.sum(
                    raised, axis=0, keepdims=True
                )
                product = jnp.dot(values, raised.astype(BF16), preferred_element_type=F32)
                summed[g, :, part] = summed[g, :, part] * factor + product

    for b in range(blocks):
        pl.when(needed[b] > 0)(functools.partial(one_block, b))
    if finish:
        for g in range(kv_heads):
            for j in range(wide // rows):
                part = slice(j * rows, (j + 1) * rows)
                result = (summed[g, :, part] * (1.0 / total[g, :, part])).T
                at = (g * (wide // rows) + j) * HEAD_DIM
                out[:, at : at + HEAD_DIM] = result.astype(BF16)


def attend(needed, queries, docs_row, docs_columns, places, keyvals, state, finish, kv_heads):
    wide = queries.shape[2]
    rows = docs_row.shape[1]
    cols = kv_heads * wide // rows * HEAD_DIM
    state_shapes = ((kv_heads, 1, wide), (kv_heads, 1, wide), (kv_heads, HEAD_DIM, wide))
    vmem = pl.BlockSpec(memory_space=pltpu.VMEM)
    smem = pl.BlockSpec(memory_space=pltpu.SMEM)
    blocks = len(keyvals)
    out_shape = (
        jax.ShapeDtypeStruct((rows, cols), BF16)
        if finish
        else tuple(jax.ShapeDtypeStruct(s, F32) for s in state_shapes)
    )
    return pl.pallas_call(
        functools.partial(
            attend_kernel,
            blocks=blocks,
            kv_heads=kv_heads,
            resume=state is not None,
            finish=finish,
        ),
        out_shape=out_shape,
        in_specs=[smem, vmem, vmem, vmem, smem] + [vmem] * (blocks + (3 if state else 0)),
        out_specs=vmem if finish else (vmem,) * 3,
        scratch_shapes=[pltpu.VMEM(s, F32) for s in state_shapes] if finish else [],
        compiler_params=params(),
        cost_estimate=cost(4 * rows * rows * cols * blocks, 4 * rows * cols),
        name="attend_rest" if finish else "attend_own",
    )(needed, queries, docs_row, docs_columns, places, *keyvals, *(state or ()))


def on_device(
    text, frames, tile_pos, frame_count, doc_ids, norm_gain, w_query, q_bias, w_key, w_value, v_bias
):
    seq_count = lax.axis_size("seq")
    vis_count = lax.axis_size("vis")
    shard = lax.axis_index("seq")
    rows, width = text.shape
    capacity = rows // (seq_count * vis_count)
    kv_heads = w_key.shape[1] // HEAD_DIM

    chunk = width // CHUNKS
    slots = make_slots(frames, norm_gain, tile_pos, frame_count, shard, rows, capacity)
    parts = swap_slots(slots, seq_count, capacity)
    pieces = assemble(parts, [chunk + META] + [chunk] * (CHUNKS - 1))
    scale = text_scale(after(text, pieces[0]))
    found = [{} for _ in pieces]
    merged, sums = [], {"total": None, "queries": q_bias.reshape(1, -1)}

    def hop(c, s, *earlier):
        for odd in (0, 1):
            pairs = hop_pairs(vis_count, s, odd)
            if pairs:
                sent = pieces[c] if s == 1 else found[c][(s - 1, 1 - odd)]
                if earlier:
                    sent = after(sent, *earlier)
                found[c][(s, odd)] = lax.ppermute(sent, "vis", pairs)
        return [found[c][(s, odd)] for odd in (0, 1) if (s, odd) in found[c]]

    def merge(c, *earlier):
        part, sums["total"] = merge_chunk(
            [pieces[0], *found[0].values()],
            [pieces[c], *found[c].values()],
            text,
            scale,
            norm_gain,
            w_key,
            w_value,
            sums["total"],
            c * chunk,
            chunk,
            v_bias if c == CHUNKS - 1 else None,
            list(earlier),
        )
        merged.append(part)

    def query(c):
        sums["queries"] = project_queries([merged[c]], w_query, c * chunk, sums["queries"], 0)

    for s in range(1, vis_count):
        for c in range(CHUNKS):
            hop(c, s)
    half = CHUNKS // 2
    for c in range(CHUNKS):
        if c == half:
            for b in range(half):
                query(b)
        merge(c, *([sums["queries"]] if c == half else []))
    keyval = sums["total"]

    queries = project_queries(
        merged[half:], w_query, half * chunk, sums["queries"], kv_heads
    )

    chips = seq_count // 2
    near, others = [(keyval, shard)], []
    for mask in range(1, chips):
        pairs = [(c, c ^ mask) for c in range(chips) if 0 < (c ^ mask) - c <= chips // 2]
        pairs = [(2 * a + core, 2 * b + core) for a, b in pairs for core in (0, 1)]
        near.append((lax.ppermute(keyval, "seq", pairs), shard ^ (2 * mask)))
    docs = doc_ids.reshape(seq_count, rows)
    docs_row = lax.dynamic_slice_in_dim(docs, shard, 1)
    docs_own = docs_row.reshape(1, rows, 1)
    core_swap = [(i, i ^ 1) for i in range(seq_count)]
    for held, origin in near:
        held = after(held, queries)
        others.append((lax.ppermute(held, "seq", core_swap), origin ^ 1))
    others += near

    origins = jnp.stack([origin for _, origin in others]).astype(jnp.int32)
    other_docs = docs[origins]
    needed = (origins <= shard) & (other_docs[:, -1] >= docs_row[0, 0])
    return attend(
        needed.astype(jnp.int32),
        queries,
        docs_row,
        other_docs.reshape(-1, rows, 1),
        (shard - origins).astype(jnp.int32) * rows,
        [entry for entry, _ in others],
        None,
        True,
        kv_heads,
    )


def solution(mesh):
    in_specs = (
        P("seq", None),
        P(("seq", "vis"), None),
        P(("seq", "vis")),
        P(("seq", "vis")),
        P(),
        P(),
        P(None, "vis"),
        P("vis"),
        P(None, "vis"),
        P(None, "vis"),
        P("vis"),
    )
    return jax.shard_map(
        on_device, mesh=mesh, in_specs=in_specs, out_specs=P("seq", "vis"), check_vma=False
    )
```

```python
import functools

import jax
import jax.numpy as jnp
from jax import lax
from jax.experimental import pallas as pl
from jax.experimental.pallas import tpu as pltpu
from jax.sharding import PartitionSpec as P

HEAD_DIM = 128
META = 128
CHUNKS = 4
EPSILON = 1e-06
NEGATIVE = -1e30
LOG2_E = 1.4426950408889634
VMEM_LIMIT = 48 * 1024 * 1024
F32 = jnp.float32
BF16 = jnp.bfloat16


def params(limit=VMEM_LIMIT):
    return pltpu.CompilerParams(vmem_limit_bytes=limit)


def cost(flops, moved):
    return pl.CostEstimate(flops=int(flops), bytes_accessed=int(moved), transcendentals=0)


def normed_rows(rows, gain):
    widened = rows.astype(F32)
    mean_square = jnp.mean(widened * widened, axis=1, keepdims=True)
    return (widened * lax.rsqrt(mean_square + EPSILON) * gain).astype(BF16)


def slots_kernel(
    scalars, frames_in, gain_in, places_in, out, frames, gain, place_row, sems, *, shard_rows, capacity
):
    fetches = [
        pltpu.make_async_copy(source, target, sems.at[i])
        for i, (source, target) in enumerate(
            ((places_in, place_row), (gain_in, gain), (frames_in, frames))
        )
    ]
    for fetch in fetches:
        fetch.start()
    for fetch in fetches:
        fetch.wait()
    count, shard = scalars[0], scalars[1]
    rows, width = frames.shape
    across = lax.broadcasted_iota(jnp.int32, (rows, rows), 1)
    down = lax.broadcasted_iota(jnp.int32, (rows, rows), 0)
    places = jnp.broadcast_to(place_row[...], (rows, rows))
    place_column = jnp.sum(jnp.where(down == across, places, 0), axis=1, keepdims=True)
    owner_row = place_row[...] // shard_rows
    owner_column = place_column // shard_rows
    same = (owner_row == owner_column) & (down < across) & (down < count)
    rank = jnp.sum(same.astype(jnp.int32), axis=0, keepdims=True)
    slot = (owner_row ^ shard) * capacity + rank
    pick = ((slot == down) & (across < count)).astype(BF16)
    local = place_column - owner_column * shard_rows + 1
    tags = jnp.broadcast_to(local.astype(F32), (rows, META)).astype(BF16)
    normed = normed_rows(frames[...], gain[...])
    lead = (out.shape[1] - META) // CHUNKS
    out[:, :lead] = jnp.dot(pick, normed[:, :lead], preferred_element_type=F32).astype(BF16)
    out[:, lead : lead + META] = jnp.dot(pick, tags, preferred_element_type=F32).astype(BF16)
    out[:, lead + META :] = jnp.dot(pick, normed[:, lead:], preferred_element_type=F32).astype(BF16)


def make_slots(frames, gain, tile_pos, frame_count, shard, shard_rows, capacity):
    rows, width = frames.shape
    scalars = jnp.stack([frame_count[0], shard.astype(jnp.int32)])
    return pl.pallas_call(
        functools.partial(slots_kernel, shard_rows=shard_rows, capacity=capacity),
        out_shape=jax.ShapeDtypeStruct((rows, width + META), BF16),
        in_specs=[pl.BlockSpec(memory_space=pltpu.SMEM)]
        + [pl.BlockSpec(memory_space=pl.ANY)] * 3,
        out_specs=pl.BlockSpec(memory_space=pltpu.VMEM),
        scratch_shapes=[
            pltpu.VMEM((rows, width), BF16),
            pltpu.VMEM((1, width), F32),
            pltpu.VMEM((1, rows), jnp.int32),
            pltpu.SemaphoreType.DMA((3,)),
        ],
        compiler_params=params(),
        cost_estimate=cost(2 * rows * rows * width, 4 * rows * width),
        name="frame_slots",
    )(scalars, frames, gain.reshape(1, width), tile_pos.reshape(1, rows))


def scale_kernel(rows, out):
    widened = rows[...].astype(F32)
    mean_square = jnp.mean(widened * widened, axis=1, keepdims=True)
    out[...] = jnp.broadcast_to(lax.rsqrt(mean_square + EPSILON), out.shape)


def text_scale(text):
    rows, width = text.shape
    step = 64
    return pl.pallas_call(
        scale_kernel,
        out_shape=jax.ShapeDtypeStruct((rows, META), F32),
        grid=(rows // step,),
        in_specs=[pl.BlockSpec((step, width), lambda i: (i, 0))],
        out_specs=pl.BlockSpec((step, META), lambda i: (i, 0)),
        compiler_params=params(),
        cost_estimate=cost(3 * rows * width, 2 * rows * width),
        name="text_scale",
    )(text)


def assemble_kernel(*refs, parts):
    at = 0
    for out in refs[parts:]:
        end = at + out.shape[1]
        found = [ref[:, at:end].astype(F32) for ref in refs[:parts]]
        out[...] = jnp.concatenate(found, axis=0).astype(BF16)
        at = end


def assemble(parts, widths):
    rows = sum(part.shape[0] for part in parts)
    if parts[0].shape[0] % 8:
        whole = jnp.concatenate(parts)
        cuts = [sum(widths[:i]) for i in range(len(widths) + 1)]
        return [whole[:, a:b] for a, b in zip(cuts, cuts[1:])]
    vmem = pl.BlockSpec(memory_space=pltpu.VMEM)
    return pl.pallas_call(
        functools.partial(assemble_kernel, parts=len(parts)),
        out_shape=[jax.ShapeDtypeStruct((rows, width), BF16) for width in widths],
        in_specs=[vmem] * len(parts),
        out_specs=[vmem] * len(widths),
        compiler_params=params(),
        cost_estimate=cost(rows * sum(widths), 4 * rows * sum(widths)),
        name="assemble",
    )(*parts)


def after(value, *earlier):
    return lax.optimization_barrier((value, earlier))[0]


def swap_slots(block, count, capacity):
    parts = [block[:capacity]]
    for d in range(1, count):
        sent = block[d * capacity : (d + 1) * capacity]
        parts.append(lax.ppermute(sent, "seq", [(i, i ^ d) for i in range(count)]))
    return parts


def hop_pairs(count, s, odd):
    links = range(odd, count - 1, 2)
    up = [(i, i + 1) for i in links if i >= s - 1]
    return up + [(i + 1, i) for i in links if i + 1 <= count - s]


def merge_kernel(*refs, blocks, rows, fresh, finish):
    tags, incoming = refs[:blocks], refs[blocks : 2 * blocks]
    text, scale, gain, w_key, w_value = refs[2 * blocks : 2 * blocks + 5]
    merged, keyval = refs[-5], refs[-4]
    total, pick, covered = refs[-3:]
    step = pl.program_id(0)
    slots = tags[0].shape[0]
    half = w_key.shape[1]

    @pl.when(step == 0)
    def _():
        places = jnp.concatenate([ref[...] for ref in tags], axis=0).astype(F32).T[:1, :]
        wanted = lax.broadcasted_iota(jnp.int32, (rows, blocks * slots), 0) + 1
        chosen = (places.astype(jnp.int32) == wanted).astype(F32)
        pick[...] = chosen.astype(BF16)
        covered[...] = jnp.broadcast_to(jnp.sum(chosen, axis=1, keepdims=True), covered.shape)
        total[...] = jnp.zeros_like(total) if fresh else refs[2 * blocks + 5][...]

    found = jnp.concatenate([ref[...] for ref in incoming], axis=0)
    placed = jnp.dot(pick[...], found, preferred_element_type=F32)
    normed = text[...].astype(F32) * scale[:, :1] * gain[...]
    rows_here = jnp.where(covered[:, :1] > 0.5, placed, normed).astype(BF16)
    merged[...] = rows_here
    total[:, :half] += jnp.dot(rows_here, w_key[...], preferred_element_type=F32)
    total[:, half:] += jnp.dot(rows_here, w_value[...], preferred_element_type=F32)

    @pl.when(step == pl.num_programs(0) - 1)
    def _():
        if finish:
            v_bias = refs[2 * blocks + 6]
            keyval[:, :half] = total[:, :half].astype(BF16)
            keyval[:, half:] = (total[:, half:] + v_bias[...]).astype(BF16)
        else:
            keyval[...] = total[...]


def merge_chunk(
    tags, incoming, text, scale, gain, w_key, w_value, total, first, width, v_bias, earlier
):
    blocks, slots = len(tags), tags[0].shape[0]
    rows = text.shape[0]
    step = 1024
    lead_step = first // step
    tag_column = width // META
    cols = w_key.shape[1]
    fresh, finish = total is None, v_bias is not None
    whole = pl.BlockSpec((rows, 2 * cols), lambda i: (0, 0))
    extra = [] if fresh else [total]
    extra_specs = [] if fresh else [whole]
    if finish:
        extra.append(v_bias.reshape(1, cols))
        extra_specs.append(pl.BlockSpec((1, cols), lambda i: (0, 0)))
    extra += earlier
    extra_specs += [pl.BlockSpec(memory_space=pl.ANY)] * len(earlier)
    return pl.pallas_call(
        functools.partial(merge_kernel, blocks=blocks, rows=rows, fresh=fresh, finish=finish),
        out_shape=(
            jax.ShapeDtypeStruct((rows, width), BF16),
            jax.ShapeDtypeStruct((rows, 2 * cols), BF16 if finish else F32),
        ),
        grid=(width // step,),
        in_specs=[pl.BlockSpec((slots, META), lambda i: (0, tag_column))] * blocks
        + [pl.BlockSpec((slots, step), lambda i: (0, i))] * blocks
        + [
            pl.BlockSpec((rows, step), lambda i: (0, i + lead_step)),
            pl.BlockSpec((rows, META), lambda i: (0, 0)),
            pl.BlockSpec((1, step), lambda i: (0, i + lead_step)),
            pl.BlockSpec((step, cols), lambda i: (i + lead_step, 0)),
            pl.BlockSpec((step, cols), lambda i: (i + lead_step, 0)),
        ]
        + extra_specs,
        out_specs=(pl.BlockSpec((rows, step), lambda i: (0, i)), whole),
        scratch_shapes=[
            pltpu.VMEM((rows, 2 * cols), F32),
            pltpu.VMEM((rows, blocks * slots), BF16),
            pltpu.VMEM((rows, META), F32),
        ],
        compiler_params=params(),
        cost_estimate=cost(
            2 * rows * width * (2 * cols + blocks * slots),
            2 * width * (blocks * slots + 2 * rows + 2 * cols),
        ),
        name="merge_rows",
    )(*tags, *incoming, text, scale, gain.reshape(1, -1), w_key, w_value, *extra)


def query_kernel(*refs, parts, finish):
    rows, (weights, bias, out) = refs[:parts], refs[parts:]
    total = bias[...]
    depth = rows[0].shape[1]
    for p in range(parts):
        total = total + jnp.dot(
            rows[p][...], weights[p * depth : (p + 1) * depth, :], preferred_element_type=F32
        )
    if finish:
        count = total.shape[0]
        for j in range(total.shape[1] // HEAD_DIM):
            head = total[:, j * HEAD_DIM : (j + 1) * HEAD_DIM]
            out[0, :, j * count : (j + 1) * count] = head.astype(BF16).T
    else:
        out[...] = total


def project_queries(parts, weights, first, earlier, groups):
    rows, depth = parts[0].shape
    cols = weights.shape[1]
    taken = depth * len(parts)
    step = 512
    out_shape = jax.ShapeDtypeStruct((rows, cols), F32)
    out_spec = pl.BlockSpec((rows, step), lambda i: (0, i))
    if groups:
        wide = cols // groups // HEAD_DIM * rows
        share = cols // groups // step
        out_shape = jax.ShapeDtypeStruct((groups, HEAD_DIM, wide), BF16)
        out_spec = pl.BlockSpec((1, HEAD_DIM, wide // share), lambda i: (i // share, 0, i % share))
    return pl.pallas_call(
        functools.partial(query_kernel, parts=len(parts), finish=groups > 0),
        out_shape=out_shape,
        grid=(cols // step,),
        in_specs=[pl.BlockSpec((rows, depth), lambda i: (0, 0))] * len(parts)
        + [
            pl.BlockSpec((taken, step), lambda i: (first // taken, i)),
            pl.BlockSpec((earlier.shape[0], step), lambda i: (0, i)),
        ],
        out_specs=out_spec,
        compiler_params=params(),
        cost_estimate=cost(2 * rows * taken * cols, 2 * (rows + cols) * taken),
        name="queries",
    )(*parts, weights, earlier)


def attend_kernel(*refs, blocks, kv_heads, resume, finish):
    needed, queries, docs_row, docs_column, places = refs[:5]
    keyvals = refs[5 : 5 + blocks]
    rest = refs[5 + blocks :]
    earlier, rest = (rest[:3], rest[3:]) if resume else (None, rest)
    out, (peak, total, summed) = (rest[0], rest[1:]) if finish else (None, rest)
    rows = docs_row.shape[1]
    wide = queries.shape[2]
    span = 8 * rows
    scale = HEAD_DIM ** (-0.5) * LOG2_E
    if resume:
        peak[...] = earlier[0][...]
        total[...] = earlier[1][...]
        summed[...] = earlier[2][...]
    else:
        peak[...] = jnp.full_like(peak, NEGATIVE)
        total[...] = jnp.zeros_like(total)
        summed[...] = jnp.zeros_like(summed)
    key_width = kv_heads * HEAD_DIM

    def one_block(b):
        down = lax.broadcasted_iota(jnp.int32, (rows, rows), 0)
        across = lax.broadcasted_iota(jnp.int32, (rows, rows), 1)
        allowed = (down - places[b] <= across) & (docs_column[b] == docs_row[...])
        bias = jnp.where(allowed, 0.0, NEGATIVE)
        bias = jnp.concatenate([bias] * (span // rows), axis=1)
        for g in range(kv_heads):
            keys = keyvals[b][:, g * HEAD_DIM : (g + 1) * HEAD_DIM]
            values = keyvals[b][:, key_width + g * HEAD_DIM : key_width + (g + 1) * HEAD_DIM].T
            for at in range(0, wide, span):
                part = slice(at, at + span)
                scores = jnp.dot(keys, queries[g, :, part], preferred_element_type=F32)
                scores = scores * scale + bias
                old = peak[g, :, part]
                new = jnp.maximum(old, jnp.max(scores, axis=0, keepdims=True))
                raised = jnp.exp2(scores - new)
                factor = jnp.exp2(old - new)
                peak[g, :, part] = new
                total[g, :, part] = total[g, :, part] * factor + jnp.sum(
                    raised, axis=0, keepdims=True
                )
                product = jnp.dot(values, raised.astype(BF16), preferred_element_type=F32)
                summed[g, :, part] = summed[g, :, part] * factor + product

    for b in range(blocks):
        pl.when(needed[b] > 0)(functools.partial(one_block, b))
    if finish:
        for g in range(kv_heads):
            for j in range(wide // rows):
                part = slice(j * rows, (j + 1) * rows)
                result = (summed[g, :, part] * (1.0 / total[g, :, part])).astype(BF16).T
                at = (g * (wide // rows) + j) * HEAD_DIM
                out[:, at : at + HEAD_DIM] = result


def attend(needed, queries, docs_row, docs_columns, places, keyvals, state, finish, kv_heads):
    wide = queries.shape[2]
    rows = docs_row.shape[1]
    cols = kv_heads * wide // rows * HEAD_DIM
    state_shapes = ((kv_heads, 1, wide), (kv_heads, 1, wide), (kv_heads, HEAD_DIM, wide))
    vmem = pl.BlockSpec(memory_space=pltpu.VMEM)
    smem = pl.BlockSpec(memory_space=pltpu.SMEM)
    blocks = len(keyvals)
    out_shape = (
        jax.ShapeDtypeStruct((rows, cols), BF16)
        if finish
        else tuple(jax.ShapeDtypeStruct(s, F32) for s in state_shapes)
    )
    return pl.pallas_call(
        functools.partial(
            attend_kernel,
            blocks=blocks,
            kv_heads=kv_heads,
            resume=state is not None,
            finish=finish,
        ),
        out_shape=out_shape,
        in_specs=[smem, vmem, vmem, vmem, smem] + [vmem] * (blocks + (3 if state else 0)),
        out_specs=vmem if finish else (vmem,) * 3,
        scratch_shapes=[pltpu.VMEM(s, F32) for s in state_shapes] if finish else [],
        compiler_params=params(),
        cost_estimate=cost(4 * rows * rows * cols * blocks, 4 * rows * cols),
        name="attend_rest" if finish else "attend_own",
    )(needed, queries, docs_row, docs_columns, places, *keyvals, *(state or ()))


def on_device(
    text, frames, tile_pos, frame_count, doc_ids, norm_gain, w_query, q_bias, w_key, w_value, v_bias
):
    seq_count = lax.axis_size("seq")
    vis_count = lax.axis_size("vis")
    shard = lax.axis_index("seq")
    rows, width = text.shape
    capacity = rows // (seq_count * vis_count)
    kv_heads = w_key.shape[1] // HEAD_DIM

    chunk = width // CHUNKS
    slots = make_slots(frames, norm_gain, tile_pos, frame_count, shard, rows, capacity)
    parts = swap_slots(slots, seq_count, capacity)
    pieces = assemble(parts, [chunk + META] + [chunk] * (CHUNKS - 1))
    scale = text_scale(after(text, pieces[0]))
    found = [{} for _ in pieces]
    merged, sums = [], {"total": None, "queries": q_bias.reshape(1, -1)}

    def hop(c, s, *earlier):
        for odd in (0, 1):
            pairs = hop_pairs(vis_count, s, odd)
            if pairs:
                sent = pieces[c] if s == 1 else found[c][(s - 1, 1 - odd)]
                if earlier:
                    sent = after(sent, *earlier)
                found[c][(s, odd)] = lax.ppermute(sent, "vis", pairs)
        return [found[c][(s, odd)] for odd in (0, 1) if (s, odd) in found[c]]

    def merge(c, *earlier):
        part, sums["total"] = merge_chunk(
            [pieces[0], *found[0].values()],
            [pieces[c], *found[c].values()],
            text,
            scale,
            norm_gain,
            w_key,
            w_value,
            sums["total"],
            c * chunk,
            chunk,
            v_bias if c == CHUNKS - 1 else None,
            list(earlier),
        )
        merged.append(part)

    def query(c):
        sums["queries"] = project_queries([merged[c]], w_query, c * chunk, sums["queries"], 0)

    for s in range(1, vis_count):
        for c in range(CHUNKS):
            hop(c, s)
    half = CHUNKS // 2
    for c in range(CHUNKS):
        if c == half:
            for b in range(half):
                query(b)
        merge(c, *([sums["queries"]] if c == half else []))
    keyval = sums["total"]

    queries = project_queries(
        merged[half:], w_query, half * chunk, sums["queries"], kv_heads
    )

    chips = seq_count // 2
    near, others = [(keyval, shard)], []
    for mask in reversed(range(1, chips)):
        pairs = [(c, c ^ mask) for c in range(chips) if abs((c ^ mask) - c) <= chips // 2]
        pairs = [(2 * a + core, 2 * b + core) for a, b in pairs for core in (0, 1)]
        near.append((lax.ppermute(keyval, "seq", pairs), shard ^ (2 * mask)))
    docs = doc_ids.reshape(seq_count, rows)
    docs_row = lax.dynamic_slice_in_dim(docs, shard, 1)
    docs_own = docs_row.reshape(1, rows, 1)
    core_swap = [(i, i ^ 1) for i in range(seq_count)]
    for held, origin in near:
        held = after(held, queries)
        others.append((lax.ppermute(held, "seq", core_swap), origin ^ 1))
    others += near

    origins = jnp.stack([origin for _, origin in others]).astype(jnp.int32)
    other_docs = docs[origins]
    needed = (origins <= shard) & (other_docs[:, -1] >= docs_row[0, 0])
    return attend(
        needed.astype(jnp.int32),
        queries,
        docs_row,
        other_docs.reshape(-1, rows, 1),
        (shard - origins).astype(jnp.int32) * rows,
        [entry for entry, _ in others],
        None,
        True,
        kv_heads,
    )


def solution(mesh):
    in_specs = (
        P("seq", None),
        P(("seq", "vis"), None),
        P(("seq", "vis")),
        P(("seq", "vis")),
        P(),
        P(),
        P(None, "vis"),
        P("vis"),
        P(None, "vis"),
        P(None, "vis"),
        P("vis"),
    )
    return jax.shard_map(
        on_device, mesh=mesh, in_specs=in_specs, out_specs=P("seq", "vis"), check_vma=False
    )
```
